32 devices in a mesh: groups: 2 (over y), row: 4 (over z), col: 4 (over x, core).
Axes of the slice: x: 2, y: 2, z: 4, core: 2. Of those that a mesh axis runs over, the one named last changes fastest.
Arguments:
- row_points: bfloat16 [32768, 512], P(('groups', 'row', 'col')), parts along dimension 0, may hold values from -8 to 8
- next_points: bfloat16 [8192, 512], P(('groups', 'row', 'col')), parts along dimension 0, may hold values from -8 to 8
- ratio: float32 [8192, 128], P(('groups', 'row', 'col')), parts along dimension 0, may hold values from 0.25 to 4
- behave_prob: float32 [8192], P(('groups', 'row', 'col')), parts along dimension 0, may hold values from 0.2 to 1
- logged_action: int32 [8192], P(('groups', 'row', 'col')), parts along dimension 0, may hold values from 0 to 3
- bucket: int32 [8192], P(('groups', 'row', 'col')), parts along dimension 0, may hold values from 0 to 63
- regime_table: int32 [128, 64], replicated, may hold values from 0 to 3
Outputs:
- proof: float32 [32768, 128], P(('groups', 'row', 'col')), parts along dimension 0
The draws below stay inside these ranges and needn't reach their ends.
There are 2 independent parts, one for each index of `groups`. The reference program is written for one: setup_inputs(seed, part) draws one part's arguments, and reference() takes and returns one part's arrays. A program takes and returns all parts, laid end to end along the dimension named above; an argument that names none is the same for every part. Nothing has to cross between parts.
All inputs are finite; a program needn't handle non-finite values.
Results may differ from the reference program's by a relative error of at most 0.0028.
Values may be sent and summed in bfloat16 or wider, within the bound.
A program may use at most 64 MiB of HBM per device.

```python
import math
import jax
import jax.numpy as jnp
from jax import lax

FEAT = 512
REGIMES = 128
ACTIONS = 4
BUCKETS = 64
STEPS = 4
TP = 1024
TQ = 256
NP = 16384
NQ = 4096
N_ROW = 4
N_COL = 4


def feature_rows(key, count):
    key_normal = jax.random.fold_in(key, 0)
    normal_part = jnp.clip(jax.random.normal(key_normal, (count, FEAT), jnp.float32), -6.0, 6.0)
    entries = normal_part
    return entries


def draw_next_points(key, part):
    nexts = feature_rows(key, NQ)
    return jnp.clip(nexts, -8.0, 8.0).astype(jnp.bfloat16)


def draw_row_points(key, part):
    nexts = feature_rows(key, NQ)
    key = jax.random.fold_in(key, 11)
    key_own, key_section, key_offset, key_level, key_noise, key_pick = jax.random.split(key, 6)
    own = feature_rows(key_own, NP)
    row_index = jnp.arange(NP, dtype=jnp.int32)
    group = row_index // (N_COL * TP)
    section = jax.random.randint(key_section, (NP,), 0, STEPS, jnp.int32)
    offset = jax.random.randint(key_offset, (NP,), 0, N_COL * TQ, jnp.int32)
    target = (group + section) % N_ROW * (N_COL * TQ) + offset
    anchors = nexts[target]
    level = jax.random.uniform(key_level, (NP, 1), jnp.float32, 3.0, 6.0)
    spread = jnp.sqrt(2.0 - 2.0 * level / math.sqrt(FEAT))
    noise = feature_rows(key_noise, NP)
    planted = anchors + spread * noise
    picked = jax.random.randint(key_pick, (NP, 1), 0, 8, jnp.int32) == 0
    rows = jnp.where(picked, planted, own)
    return jnp.clip(rows, -8.0, 8.0).astype(jnp.bfloat16)


def with_ends(result, stream_key, least, high):
    spot = [jax.random.randint(jax.random.fold_in(stream_key, axis), (), 0, length) for axis, length in enumerate(result.shape)]
    main_axis = result.shape.index(max(result.shape))
    beside = spot[:main_axis] + [(spot[main_axis] + 1) % result.shape[main_axis]] + spot[main_axis + 1:]
    return result.at[tuple(spot)].set(least).at[tuple(beside)].set(high)


def shard_levels(stream_key, dims, pieces, low, largest):
    factor_of, own = 1.0, jax.random.fold_in(stream_key, 6)
    for position, shards_of in pieces:
        steps = jnp.exp(jax.random.uniform(jax.random.fold_in(own, position), (shards_of,), jnp.float32, low / len(pieces), largest / len(pieces)))
        factor_of = factor_of * jnp.repeat(steps, dims[position] // shards_of).reshape([-1 if axis == position else 1 for axis in range(len(dims))])
    return factor_of


def setup_inputs(seed: int = 0, part: int = 0) -> dict:
    key_of = jax.random.split(jax.random.key(seed), 8)
    part_keys = jax.random.split(jax.random.fold_in(key_of[7], part), 8)
    return {
        "row_points": draw_row_points(jax.random.fold_in(jax.random.fold_in(key_of[7], part), 71), part),
        "next_points": draw_next_points(jax.random.fold_in(jax.random.fold_in(key_of[7], part), 71), part),
        "ratio": jnp.clip(jnp.exp(math.log(4.0) - 2.7725887 * jax.random.uniform(part_keys[2], (NQ, REGIMES), jnp.float32) ** shard_levels(part_keys[2], (NQ, REGIMES), ((0, 16),), -0.2, 0.2)), 0.25, 4.0),
        "behave_prob": jnp.clip(jnp.exp(math.log(1.0) - 1.609438 * jax.random.uniform(part_keys[3], (NQ,), jnp.float32) ** shard_levels(part_keys[3], (NQ,), ((0, 16),), -0.2, 0.2)), 0.2, 1.0),
        "logged_action": with_ends(jax.random.randint(part_keys[4], (NQ,), 0, ACTIONS), jax.random.fold_in(part_keys[4], 1), 0, ACTIONS - 1).astype(jnp.int32),
        "bucket": with_ends(jax.random.randint(part_keys[5], (NQ,), 0, BUCKETS), jax.random.fold_in(part_keys[5], 1), 0, BUCKETS - 1).astype(jnp.int32),
        "regime_table": with_ends(jax.random.randint(key_of[6], (REGIMES, BUCKETS), 0, ACTIONS), jax.random.fold_in(key_of[6], 1), 0, ACTIONS - 1).astype(jnp.int32),
    }


KERNEL_SCALE = 0.5
DISCOUNT = 0.9

def residual_block(ratio, behave_prob, logged_action, bucket, regime_table):
    onehot = (bucket[:, None] == jnp.arange(BUCKETS, dtype=jnp.int32)[None, :]).astype(jnp.float32)
    chosen = jnp.dot(onehot, regime_table.astype(jnp.float32).T, precision=lax.Precision.HIGHEST)
    matched = (chosen == logged_action.astype(jnp.float32)[:, None]).astype(jnp.float32)
    importance = matched / behave_prob[:, None]
    return ((DISCOUNT * importance - 1.0) * ratio).astype(jnp.bfloat16)

def kernel_tile(row_block, row_norm, column_block):
    features = row_block.shape[1]
    columns = column_block[:, :features]
    residual = column_block[:, features:]
    column_norm = lax.optimization_barrier(jnp.sum(jnp.square(columns.astype(jnp.float32)), axis=1))
    inner_terms = lax.dot_general(row_block, columns, (((1,), (1,)), ((), ())), preferred_element_type=jnp.float32)
    coefficient = KERNEL_SCALE / math.sqrt(features)
    exponent = coefficient * (2.0 * inner_terms - row_norm[:, None] - column_norm[None, :] + 2.0 * features)
    kernel = jnp.exp(exponent).astype(jnp.bfloat16)
    return jnp.dot(kernel, residual, preferred_element_type=jnp.float32)

def reference(row_points, next_points, ratio, behave_prob, logged_action, bucket, regime_table):
    residual = residual_block(ratio, behave_prob, logged_action, bucket, regime_table)
    packed = jnp.concatenate([next_points, residual], axis=1).reshape(N_ROW, N_COL * TQ, FEAT + REGIMES)
    groups_rows = row_points.reshape(N_ROW, N_COL * TP, FEAT)

    def one_group(group_index):
        row_block = lax.dynamic_index_in_dim(groups_rows, group_index, 0, keepdims=False)
        row_norm = lax.optimization_barrier(jnp.sum(jnp.square(row_block.astype(jnp.float32)), axis=1))
        summed = jnp.zeros((N_COL * TP, REGIMES), jnp.float32)
        for section in range(STEPS):
            column_block = lax.dynamic_index_in_dim(packed, ((group_index + section) % N_ROW).astype(jnp.int32), 0, keepdims=False)
            summed = summed + kernel_tile(row_block, row_norm, column_block)
        return summed
    proof = lax.map(one_group, jnp.arange(N_ROW, dtype=jnp.int32))
    return proof.reshape(NP, REGIMES) / float(STEPS * N_COL * TQ)
```

```python
import functools
import math

import jax
import jax.numpy as jnp
from jax import lax
from jax.experimental import pallas as pl
from jax.experimental.pallas import tpu as pltpu
from jax.sharding import PartitionSpec as P

BUCKETS = 64
STEPS = 4


KERNEL_SCALE = 0.5
DISCOUNT = 0.9


def passed_along(block, axis, distance):
    devices = range(lax.axis_size(axis))
    route = [((i - distance) % len(devices), i) for i in devices]
    return lax.ppermute(block, axis, route)


def residual_block(ratio, behave_prob, logged_action, bucket, regime_table):
    onehot = (bucket[:, None] == jnp.arange(BUCKETS, dtype=jnp.int32)[None, :]).astype(jnp.float32)
    chosen = jnp.dot(onehot, regime_table.astype(jnp.float32).T, precision=lax.Precision.HIGHEST)
    matched = (chosen == logged_action.astype(jnp.float32)[:, None]).astype(jnp.float32)
    importance = matched / behave_prob[:, None]
    return ((DISCOUNT * importance - 1.0) * ratio).astype(jnp.bfloat16)


def kernel_tile(row_block, row_norm, column_block):
    features = row_block.shape[1]
    columns = column_block[:, :features]
    residual = column_block[:, features:]
    column_norm = jnp.sum(jnp.square(columns.astype(jnp.float32)), axis=1)
    inner_terms = lax.dot_general(
        row_block, columns, (((1,), (1,)), ((), ())), preferred_element_type=jnp.float32
    )
    coefficient = KERNEL_SCALE / math.sqrt(features)
    exponent = coefficient * (
        2.0 * inner_terms - row_norm[:, None] - column_norm[None, :] + 2.0 * features
    )
    kernel = jnp.exp(exponent).astype(jnp.bfloat16)
    return jnp.dot(kernel, residual, preferred_element_type=jnp.float32)


def gathered_body(row_points, next_points, ratio, behave_prob, logged_action, bucket, regime_table):
    residual = residual_block(ratio, behave_prob, logged_action, bucket, regime_table)
    packed = jnp.concatenate([next_points, residual], axis=1)
    row_norm = jnp.sum(jnp.square(row_points.astype(jnp.float32)), axis=1)
    col_count = lax.axis_size("col")
    local_rows = next_points.shape[0]
    summed = jnp.zeros((row_points.shape[0], ratio.shape[1]), jnp.float32)
    pieces = [packed]
    for offset in range(1, STEPS):
        pieces.append(passed_along(packed, "row", -offset))
    stacked = jnp.stack(pieces, axis=0)
    gathered = lax.all_gather(stacked, "col", axis=1, tiled=True)
    for section in range(STEPS):
        summed = summed + kernel_tile(row_points, row_norm, gathered[section])
    return summed / float(STEPS * col_count * local_rows)


SUBS = 2
PARTNER, ACROSS, BESIDE, SIBLING = range(4)


def interleaved(*lists):
    merged = []
    for order, entries in enumerate(lists):
        merged += [(place, order, entry) for place, entry in enumerate(entries)]
    return [entry for _, _, entry in sorted(merged, key=lambda item: item[:2])]


def arrivals(subs):
    half = subs // 2
    every = list(range(subs))

    def block(other_column, end, other_side, parts, *directions):
        return [(other_column, end, other_side, part, directions + (SIBLING,)) for part in parts]

    at_end = interleaved(
        block(0, 0, 0, every[:half], BESIDE)
        + block(0, 0, 0, every[half:])
        + block(0, 0, 1, every, BESIDE)
        + block(0, 1, 1, every, BESIDE)
        + block(1, 0, 0, every[half:]),
        block(1, 1, 0, every, PARTNER)
        + block(1, 0, 0, every[:half])
        + block(1, 0, 1, every)
        + block(1, 1, 1, every),
    )
    at_middle = interleaved(
        block(0, 0, 1, every, PARTNER, BESIDE) + block(0, 1, 1, every, PARTNER, BESIDE),
        block(0, 1, 0, every, ACROSS) + block(1, 1, 0, every),
        block(1, 0, 0, every[half:], PARTNER)
        + block(1, 0, 0, every[:half])
        + block(1, 0, 1, every)
        + block(1, 1, 1, every),
    )
    return at_end, at_middle


def proof_kernel(
    scale, rows_ref, next_ref, ratio_ref, behave_ref, action_ref, bucket_ref, table_ref, out_ref,
    held, row_term, send_sem, recv_sem,
):
    z, col = lax.axis_index("row"), lax.axis_index("col")
    x, core = col // 2, col % 2
    is_end = (z == 0) | (z == 3)
    is_middle = jnp.logical_not(is_end)
    side = z // 2
    shard, features = next_ref.shape
    sub_rows = shard // SUBS
    width = 2 * sub_rows
    partner = z + 1 - 2 * (z % 2)
    target = {
        PARTNER: (partner, col),
        ACROSS: (3 - z, col),
        BESIDE: (z, (1 - x) * 2 + core),
        SIBLING: (z, x * 2 + 1 - core),
    }

    def device(direction):
        to_row, to_col = target[direction]
        return {"row": to_row, "col": to_col}

    def unit_of(other_column, end, other_side, sub):
        bx = (1 - x) if other_column else x
        bside = (1 - side) if other_side else side
        bz = 3 * bside if end else 1 + bside
        return (bx * 4 + bz) * SUBS + sub

    def part(unit, of_core):
        return held.at[pl.ds(pl.multiple_of((unit * 2 + of_core) * sub_rows, sub_rows), sub_rows), :]

    def transfer(unit, of_core, direction):
        return pltpu.make_async_remote_copy(
            src_ref=part(unit, of_core),
            dst_ref=part(unit, of_core),
            send_sem=send_sem.at[unit, direction],
            recv_sem=recv_sem.at[unit * 2 + of_core],
            device_id=device(direction),
            device_id_type=pl.DeviceIdType.MESH,
        )

    barrier = pltpu.get_barrier_semaphore()

    def greet(direction):
        pl.semaphore_signal(
            barrier, inc=1, device_id=device(direction), device_id_type=pl.DeviceIdType.MESH
        )

    greet(PARTNER)
    greet(BESIDE)
    greet(SIBLING)

    @pl.when(is_middle)
    def _():
        greet(ACROSS)

    mine = (x * 4 + z) * SUBS
    columns = jnp.concatenate(
        [
            bucket_ref[...].astype(jnp.float32),
            action_ref[...].astype(jnp.float32),
            behave_ref[...],
            jnp.zeros((5, shard), jnp.float32),
        ],
        axis=0,
    ).T
    buckets = table_ref.shape[1]
    onehot = (columns[:, 0:1] == lax.broadcasted_iota(jnp.int32, (shard, buckets), 1).astype(jnp.float32))
    chosen = lax.dot_general(
        onehot.astype(jnp.float32).astype(jnp.bfloat16),
        table_ref[...].astype(jnp.float32).astype(jnp.bfloat16),
        (((1,), (1,)), ((), ())),
        preferred_element_type=jnp.float32,
    )
    matched = jnp.where(chosen == columns[:, 1:2], 1.0, 0.0)
    importance = matched / columns[:, 2:3]
    residual = ((DISCOUNT * importance - 1.0) * ratio_ref[...]).astype(jnp.bfloat16)
    for sub in range(SUBS):
        own = part(mine + sub, core)
        own[:, :features] = next_ref[sub * sub_rows:(sub + 1) * sub_rows, :]
        own[:, features:] = residual[sub * sub_rows:(sub + 1) * sub_rows, :]

    pl.semaphore_wait(barrier, jnp.where(is_end, 3, 4))

    half = SUBS // 2
    for sub in range(SUBS):
        for direction in (PARTNER, SIBLING):
            transfer(mine + sub, core, direction).start()

        @pl.when(is_end)
        def _():
            transfer(mine + sub, core, BESIDE).start()

        @pl.when(is_middle)
        def _():
            transfer(mine + sub, core, ACROSS).start()
            transfer(mine + (sub + half) % SUBS, core, BESIDE).start()

    fold = KERNEL_SCALE / math.sqrt(features) * math.log2(math.e)
    row_count = rows_ref.shape[0]
    tile = min(256, row_count)

    @pl.loop(0, row_count // tile)
    def _(step):
        here = pl.ds(pl.multiple_of(step * tile, tile), tile)
        squares = jnp.square(rows_ref[here, :].astype(jnp.float32))
        row_term[here, :] = fold * (2.0 * features - jnp.sum(squares, axis=1, keepdims=True))
        out_ref[here, :] = jnp.zeros((tile, out_ref.shape[1]), jnp.float32)

    def add_unit(unit):
        start = pl.ds(pl.multiple_of(unit * width, width), width)
        points = held[start, :features]
        weights = held[start, features:]
        squares = jnp.square(points.astype(jnp.float32))
        high = squares.astype(jnp.bfloat16)
        low = (squares - high.astype(jnp.float32)).astype(jnp.bfloat16)
        ones = jnp.ones((16, features), jnp.bfloat16)
        contract = (((1,), (1,)), ((), ()))
        norm = lax.dot_general(ones, high, contract, preferred_element_type=jnp.float32)
        norm += lax.dot_general(ones, low, contract, preferred_element_type=jnp.float32)
        column_term = fold * norm[0:1, :]

        @pl.loop(0, row_count // tile)
        def _(step):
            here = pl.ds(pl.multiple_of(step * tile, tile), tile)
            inner = lax.dot_general(
                rows_ref[here, :], points, contract, preferred_element_type=jnp.float32
            )
            exponent = (2.0 * fold) * inner + (row_term[here, :] - column_term)
            kernel = jnp.exp2(exponent).astype(jnp.bfloat16)
            out_ref[here, :] += jnp.dot(kernel, weights, preferred_element_type=jnp.float32)

    waiting = [mine + sub for sub in range(SUBS)]

    def add_oldest():
        unit = waiting.pop(0)
        transfer(unit, 1 - core, SIBLING).wait_recv()
        add_unit(unit)

    at_end, at_middle = arrivals(SUBS)
    passed = []
    for end_entry, middle_entry in zip(at_end, at_middle, strict=True):
        unit = jnp.where(is_end, unit_of(*end_entry[:4]), unit_of(*middle_entry[:4]))
        transfer(unit, core, SIBLING).wait_recv()
        for direction in (BESIDE, PARTNER, ACROSS, SIBLING):
            in_end, in_middle = direction in end_entry[4], direction in middle_entry[4]
            if in_end and in_middle:
                transfer(unit, core, direction).start()
            elif in_end or in_middle:

                @pl.when(is_end if in_end else is_middle)
                def _():
                    transfer(unit, core, direction).start()

            passed.append((unit, direction, in_end, in_middle))
        waiting.append(unit)
        if len(waiting) > 1:
            add_oldest()
    while waiting:
        add_oldest()

    @pl.loop(0, row_count // tile)
    def _(step):
        here = pl.ds(pl.multiple_of(step * tile, tile), tile)
        out_ref[here, :] = out_ref[here, :] / scale

    for sub in range(SUBS):
        for direction in (PARTNER, BESIDE, SIBLING):
            transfer(mine + sub, core, direction).wait_send()

        @pl.when(is_middle)
        def _():
            transfer(mine + sub, core, ACROSS).wait_send()

    for unit, direction, in_end, in_middle in passed:
        if in_end and in_middle:
            transfer(unit, core, direction).wait_send()
        elif in_end or in_middle:

            @pl.when(is_end if in_end else is_middle)
            def _():
                transfer(unit, core, direction).wait_send()


def relayed_body(row_points, next_points, ratio, behave_prob, logged_action, bucket, regime_table):
    rows, features = row_points.shape
    shard, regimes = ratio.shape
    devices = lax.axis_size("row") * lax.axis_size("col")
    columns = devices * shard
    units = devices // 2 * SUBS
    return pl.pallas_call(
        functools.partial(proof_kernel, float(columns)),
        out_shape=jax.ShapeDtypeStruct((rows, regimes), jnp.float32),
        in_specs=[pl.BlockSpec(memory_space=pltpu.VMEM)] * 7,
        out_specs=pl.BlockSpec(memory_space=pltpu.VMEM),
        scratch_shapes=[
            pltpu.VMEM((columns, features + regimes), jnp.bfloat16),
            pltpu.VMEM((rows, 1), jnp.float32),
            pltpu.SemaphoreType.DMA((units, 4)),
            pltpu.SemaphoreType.DMA((units * 2,)),
        ],
        compiler_params=pltpu.CompilerParams(
            collective_id=0, has_side_effects=True, vmem_limit_bytes=40 * 2**20
        ),
    )(
        row_points,
        next_points,
        ratio,
        behave_prob.reshape(1, shard),
        logged_action.reshape(1, shard),
        bucket.reshape(1, shard),
        regime_table,
    )


def solution(mesh):
    whole_window = mesh.shape["row"] == STEPS == 4 and mesh.shape["col"] == 4
    body = relayed_body if whole_window else gathered_body
    placed = (
        P(("groups", "row", "col"), None),
        P(("groups", "row", "col"), None),
        P(("groups", "row", "col"), None),
        P(("groups", "row", "col")),
        P(("groups", "row", "col")),
        P(("groups", "row", "col")),
        P(),
    )
    return jax.shard_map(
        body,
        mesh=mesh,
        in_specs=placed,
        out_specs=P(("groups", "row", "col"), None),
        check_vma=False,
    )
```

```python
import functools
import math

import jax
import jax.numpy as jnp
from jax import lax
from jax.experimental import pallas as pl
from jax.experimental.pallas import tpu as pltpu
from jax.sharding import PartitionSpec as P

BUCKETS = 64
STEPS = 4


KERNEL_SCALE = 0.5
DISCOUNT = 0.9


def passed_along(block, axis, distance):
    devices = range(lax.axis_size(axis))
    route = [((i - distance) % len(devices), i) for i in devices]
    return lax.ppermute(block, axis, route)


def residual_block(ratio, behave_prob, logged_action, bucket, regime_table):
    onehot = (bucket[:, None] == jnp.arange(BUCKETS, dtype=jnp.int32)[None, :]).astype(jnp.float32)
    chosen = jnp.dot(onehot, regime_table.astype(jnp.float32).T, precision=lax.Precision.HIGHEST)
    matched = (chosen == logged_action.astype(jnp.float32)[:, None]).astype(jnp.float32)
    importance = matched / behave_prob[:, None]
    return ((DISCOUNT * importance - 1.0) * ratio).astype(jnp.bfloat16)


def kernel_tile(row_block, row_norm, column_block):
    features = row_block.shape[1]
    columns = column_block[:, :features]
    residual = column_block[:, features:]
    column_norm = jnp.sum(jnp.square(columns.astype(jnp.float32)), axis=1)
    inner_terms = lax.dot_general(
        row_block, columns, (((1,), (1,)), ((), ())), preferred_element_type=jnp.float32
    )
    coefficient = KERNEL_SCALE / math.sqrt(features)
    exponent = coefficient * (
        2.0 * inner_terms - row_norm[:, None] - column_norm[None, :] + 2.0 * features
    )
    kernel = jnp.exp(exponent).astype(jnp.bfloat16)
    return jnp.dot(kernel, residual, preferred_element_type=jnp.float32)


def gathered_body(row_points, next_points, ratio, behave_prob, logged_action, bucket, regime_table):
    residual = residual_block(ratio, behave_prob, logged_action, bucket, regime_table)
    packed = jnp.concatenate([next_points, residual], axis=1)
    row_norm = jnp.sum(jnp.square(row_points.astype(jnp.float32)), axis=1)
    col_count = lax.axis_size("col")
    local_rows = next_points.shape[0]
    summed = jnp.zeros((row_points.shape[0], ratio.shape[1]), jnp.float32)
    pieces = [packed]
    for offset in range(1, STEPS):
        pieces.append(passed_along(packed, "row", -offset))
    stacked = jnp.stack(pieces, axis=0)
    gathered = lax.all_gather(stacked, "col", axis=1, tiled=True)
    for section in range(STEPS):
        summed = summed + kernel_tile(row_points, row_norm, gathered[section])
    return summed / float(STEPS * col_count * local_rows)


SUBS = 4
PARTNER, ACROSS, BESIDE, SIBLING = range(4)


def interleaved(*lists):
    merged = []
    for order, entries in enumerate(lists):
        merged += [(place, order, entry) for place, entry in enumerate(entries)]
    return [entry for _, _, entry in sorted(merged, key=lambda item: item[:2])]


def arrivals(subs):
    half = subs // 2
    every = list(range(subs))

    def block(other_column, end, other_side, parts, *directions):
        return [(other_column, end, other_side, part, directions + (SIBLING,)) for part in parts]

    at_end = interleaved(
        block(0, 0, 0, every[:half], BESIDE)
        + block(0, 0, 0, every[half:])
        + block(0, 0, 1, every, BESIDE)
        + block(0, 1, 1, every, BESIDE)
        + block(1, 0, 0, every[half:]),
        block(1, 1, 0, every, PARTNER)
        + block(1, 0, 0, every[:half])
        + block(1, 0, 1, every)
        + block(1, 1, 1, every),
    )
    at_middle = interleaved(
        block(0, 0, 1, every, PARTNER, BESIDE) + block(0, 1, 1, every, PARTNER, BESIDE),
        block(0, 1, 0, every, ACROSS) + block(1, 1, 0, every),
        block(1, 0, 0, every[half:], PARTNER)
        + block(1, 0, 0, every[:half])
        + block(1, 0, 1, every)
        + block(1, 1, 1, every),
    )
    return at_end, at_middle


def complete_groups(entries, group):
    count, found = {}, []
    for step, (other_column, end, other_side, sub, _) in enumerate(entries):
        key = (other_column, end, other_side, sub // group * group)
        count[key] = count.get(key, 0) + 1
        if count[key] == group:
            found.append((step,) + key)
    return found


def proof_kernel(
    rows_hbm, next_hbm, ratio_hbm, behave_ref, action_ref, bucket_ref, table_ref, out_ref,
    held, rows_ref, ratio_ref, row_term, local_sem, send_sem, recv_sem,
):
    z, col = lax.axis_index("row"), lax.axis_index("col")
    x, core = col // 2, col % 2
    is_end = (z == 0) | (z == 3)
    is_middle = jnp.logical_not(is_end)
    side = z // 2
    shard, features = next_hbm.shape
    sub_rows = shard // SUBS
    group = SUBS // 2
    width = 2 * group * sub_rows
    partner = z + 1 - 2 * (z % 2)
    target = {
        PARTNER: (partner, col),
        ACROSS: (3 - z, col),
        BESIDE: (z, (1 - x) * 2 + core),
        SIBLING: (z, x * 2 + 1 - core),
    }

    def device(direction):
        to_row, to_col = target[direction]
        return {"row": to_row, "col": to_col}

    def unit_of(other_column, end, other_side, sub):
        bx = (1 - x) if other_column else x
        bside = (1 - side) if other_side else side
        bz = 3 * bside if end else 1 + bside
        return (bx * 4 + bz) * SUBS + sub

    def part(unit, of_core):
        return held.at[pl.ds(pl.multiple_of((unit * 2 + of_core) * sub_rows, sub_rows), sub_rows), :]

    def transfer(unit, of_core, direction):
        return pltpu.make_async_remote_copy(
            src_ref=part(unit, of_core),
            dst_ref=part(unit, of_core),
            send_sem=send_sem.at[unit, direction],
            recv_sem=recv_sem.at[unit * 2 + of_core],
            device_id=device(direction),
            device_id_type=pl.DeviceIdType.MESH,
        )

    barrier = pltpu.get_barrier_semaphore()

    def greet(direction):
        pl.semaphore_signal(
            barrier, inc=1, device_id=device(direction), device_id_type=pl.DeviceIdType.MESH
        )

    greet(PARTNER)
    greet(BESIDE)
    greet(SIBLING)

    @pl.when(is_middle)
    def _():
        greet(ACROSS)

    mine = (x * 4 + z) * SUBS
    ratio_copy = pltpu.make_async_copy(ratio_hbm, ratio_ref, local_sem.at[0])
    ratio_copy.start()
    next_copies = []
    for sub in range(SUBS):
        next_copies.append(
            pltpu.make_async_copy(
                next_hbm.at[pl.ds(sub * sub_rows, sub_rows), :],
                part(mine + sub, core).at[:, pl.ds(0, features)],
                local_sem.at[2 + sub],
            )
        )
        next_copies[sub].start()
    rows_copy = pltpu.make_async_copy(rows_hbm, rows_ref, local_sem.at[1])
    rows_copy.start()
    columns = jnp.concatenate(
        [
            bucket_ref[...].astype(jnp.float32),
            action_ref[...].astype(jnp.float32),
            behave_ref[...],
            jnp.zeros((5, shard), jnp.float32),
        ],
        axis=0,
    ).T
    buckets = table_ref.shape[0]
    onehot = (columns[:, 0:1] == lax.broadcasted_iota(jnp.int32, (shard, buckets), 1).astype(jnp.float32))
    chosen = lax.dot_general(
        onehot.astype(jnp.float32).astype(jnp.bfloat16),
        table_ref[...].astype(jnp.float32).astype(jnp.bfloat16),
        (((1,), (0,)), ((), ())),
        preferred_element_type=jnp.float32,
    )
    matched = jnp.where(chosen == columns[:, 1:2], 1.0, 0.0)
    importance = matched / columns[:, 2:3]
    ratio_copy.wait()
    residual = ((DISCOUNT * importance - 1.0) * ratio_ref[...]).astype(jnp.bfloat16)
    for sub in range(SUBS):
        own = part(mine + sub, core)
        own[:, features:] = residual[sub * sub_rows:(sub + 1) * sub_rows, :]

    for copy in next_copies:
        copy.wait()
    pl.semaphore_wait(barrier, jnp.where(is_end, 3, 4))

    half = SUBS // 2
    for sub in range(SUBS):
        for direction in (PARTNER, SIBLING):
            transfer(mine + sub, core, direction).start()

        @pl.when(is_end)
        def _():
            transfer(mine + sub, core, BESIDE).start()

        @pl.when(is_middle)
        def _():
            transfer(mine + sub, core, ACROSS).start()
            transfer(mine + (sub + half) % SUBS, core, BESIDE).start()

    fold = KERNEL_SCALE / math.sqrt(features) * math.log2(math.e)
    rows_copy.wait()
    row_count = rows_ref.shape[0]
    tile = min(256, row_count)

    @pl.loop(0, row_count // tile)
    def _(step):
        here = pl.ds(pl.multiple_of(step * tile, tile), tile)
        squares = jnp.square(rows_ref[here, :].astype(jnp.float32))
        row_term[here, :] = fold * (2.0 * features - jnp.sum(squares, axis=1, keepdims=True))
        out_ref[here, :] = jnp.zeros((tile, out_ref.shape[1]), jnp.float32)

    def add_group(unit):
        start = pl.ds(pl.multiple_of(unit * 2 * sub_rows, width), width)
        points = held[start, :features]
        weights = held[start, features:]
        squares = jnp.square(points.astype(jnp.float32))
        lanes = functools.reduce(
            jnp.add, [squares[:, at:at + 128] for at in range(0, features, 128)]
        )
        column_term = fold * jnp.sum(lanes.T, axis=0, keepdims=True)
        inner = lax.dot_general(
            rows_ref[...], points, (((1,), (1,)), ((), ())), preferred_element_type=jnp.float32
        )
        exponent = (2.0 * fold) * inner + (row_term[...] - column_term)
        kernel = jnp.exp2(exponent).astype(jnp.bfloat16)
        out_ref[...] += jnp.dot(kernel, weights, preferred_element_type=jnp.float32)

    at_end, at_middle = arrivals(SUBS)
    groups_of_end, groups_of_middle = complete_groups(at_end, group), complete_groups(at_middle, group)
    for at in range(0, SUBS, group):
        for sub in range(at, at + group):
            transfer(mine + sub, 1 - core, SIBLING).wait_recv()
        add_group(mine + at)

    passed = []
    done = 0
    for step, (end_entry, middle_entry) in enumerate(zip(at_end, at_middle, strict=True)):
        unit = jnp.where(is_end, unit_of(*end_entry[:4]), unit_of(*middle_entry[:4]))
        transfer(unit, core, SIBLING).wait_recv()
        for direction in (BESIDE, PARTNER, ACROSS, SIBLING):
            in_end, in_middle = direction in end_entry[4], direction in middle_entry[4]
            if in_end and in_middle:
                transfer(unit, core, direction).start()
            elif in_end or in_middle:

                @pl.when(is_end if in_end else is_middle)
                def _():
                    transfer(unit, core, direction).start()

            passed.append((unit, direction, in_end, in_middle))
        last = step == len(at_end) - 1
        while done < len(groups_of_end):
            (end_step, *of_end), (middle_step, *of_middle) = groups_of_end[done], groups_of_middle[done]
            if not last and max(end_step, middle_step) >= step:
                break
            first = jnp.where(is_end, unit_of(*of_end), unit_of(*of_middle))
            for sub in range(group):
                transfer(first + sub, 1 - core, SIBLING).wait_recv()
            add_group(first)
            done += 1

    for sub in range(SUBS):
        for direction in (PARTNER, BESIDE, SIBLING):
            transfer(mine + sub, core, direction).wait_send()

        @pl.when(is_middle)
        def _():
            transfer(mine + sub, core, ACROSS).wait_send()

    for unit, direction, in_end, in_middle in passed:
        if in_end and in_middle:
            transfer(unit, core, direction).wait_send()
        elif in_end or in_middle:

            @pl.when(is_end if in_end else is_middle)
            def _():
                transfer(unit, core, direction).wait_send()


def relayed_body(row_points, next_points, ratio, behave_prob, logged_action, bucket, regime_table):
    rows, features = row_points.shape
    shard, regimes = ratio.shape
    devices = lax.axis_size("row") * lax.axis_size("col")
    columns = devices * shard
    units = devices // 2 * SUBS
    total = pl.pallas_call(
        proof_kernel,
        out_shape=jax.ShapeDtypeStruct((rows, regimes), jnp.float32),
        in_specs=[pl.BlockSpec(memory_space=pltpu.HBM)] * 3
        + [pl.BlockSpec(memory_space=pltpu.VMEM)] * 4,
        out_specs=pl.BlockSpec(memory_space=pltpu.VMEM),
        scratch_shapes=[
            pltpu.VMEM((columns, features + regimes), jnp.bfloat16),
            pltpu.VMEM((rows, features), jnp.bfloat16),
            pltpu.VMEM((shard, regimes), jnp.float32),
            pltpu.VMEM((rows, 1), jnp.float32),
            pltpu.SemaphoreType.DMA((2 + SUBS,)),
            pltpu.SemaphoreType.DMA((units, 4)),
            pltpu.SemaphoreType.DMA((units * 2,)),
        ],
        compiler_params=pltpu.CompilerParams(
            collective_id=0, has_side_effects=True, vmem_limit_bytes=60 * 2**20
        ),
    )(
        row_points,
        next_points,
        ratio,
        behave_prob.reshape(1, shard),
        logged_action.reshape(1, shard),
        bucket.reshape(1, shard),
        regime_table.T,
    )
    return total / float(columns)


def solution(mesh):
    whole_window = mesh.shape["row"] == STEPS == 4 and mesh.shape["col"] == 4
    body = relayed_body if whole_window else gathered_body
    placed = (
        P(("groups", "row", "col"), None),
        P(("groups", "row", "col"), None),
        P(("groups", "row", "col"), None),
        P(("groups", "row", "col")),
        P(("groups", "row", "col")),
        P(("groups", "row", "col")),
        P(),
    )
    return jax.shard_map(
        body,
        mesh=mesh,
        in_specs=placed,
        out_specs=P(("groups", "row", "col"), None),
        check_vma=False,
    )
```

```python
import functools
import math

import jax
import jax.numpy as jnp
from jax import lax
from jax.experimental import pallas as pl
from jax.experimental.pallas import tpu as pltpu
from jax.sharding import PartitionSpec as P

BUCKETS = 64
STEPS = 4


KERNEL_SCALE = 0.5
DISCOUNT = 0.9


def passed_along(block, axis, distance):
    devices = range(lax.axis_size(axis))
    route = [((i - distance) % len(devices), i) for i in devices]
    return lax.ppermute(block, axis, route)


def residual_block(ratio, behave_prob, logged_action, bucket, regime_table):
    onehot = (bucket[:, None] == jnp.arange(BUCKETS, dtype=jnp.int32)[None, :]).astype(jnp.float32)
    chosen = jnp.dot(onehot, regime_table.astype(jnp.float32).T, precision=lax.Precision.HIGHEST)
    matched = (chosen == logged_action.astype(jnp.float32)[:, None]).astype(jnp.float32)
    importance = matched / behave_prob[:, None]
    return ((DISCOUNT * importance - 1.0) * ratio).astype(jnp.bfloat16)


def kernel_tile(row_block, row_norm, column_block):
    features = row_block.shape[1]
    columns = column_block[:, :features]
    residual = column_block[:, features:]
    column_norm = jnp.sum(jnp.square(columns.astype(jnp.float32)), axis=1)
    inner_terms = lax.dot_general(
        row_block, columns, (((1,), (1,)), ((), ())), preferred_element_type=jnp.float32
    )
    coefficient = KERNEL_SCALE / math.sqrt(features)
    exponent = coefficient * (
        2.0 * inner_terms - row_norm[:, None] - column_norm[None, :] + 2.0 * features
    )
    kernel = jnp.exp(exponent).astype(jnp.bfloat16)
    return jnp.dot(kernel, residual, preferred_element_type=jnp.float32)


def gathered_body(row_points, next_points, ratio, behave_prob, logged_action, bucket, regime_table):
    residual = residual_block(ratio, behave_prob, logged_action, bucket, regime_table)
    packed = jnp.concatenate([next_points, residual], axis=1)
    row_norm = jnp.sum(jnp.square(row_points.astype(jnp.float32)), axis=1)
    col_count = lax.axis_size("col")
    local_rows = next_points.shape[0]
    summed = jnp.zeros((row_points.shape[0], ratio.shape[1]), jnp.float32)
    pieces = [packed]
    for offset in range(1, STEPS):
        pieces.append(passed_along(packed, "row", -offset))
    stacked = jnp.stack(pieces, axis=0)
    gathered = lax.all_gather(stacked, "col", axis=1, tiled=True)
    for section in range(STEPS):
        summed = summed + kernel_tile(row_points, row_norm, gathered[section])
    return summed / float(STEPS * col_count * local_rows)


SUBS = 4
MIDDLE_BESIDE = 3
PARTNER, ACROSS, BESIDE, SIBLING = range(4)


def interleaved(*lists):
    merged = []
    for order, entries in enumerate(lists):
        merged += [(place, order, entry) for place, entry in enumerate(entries)]
    return [entry for _, _, entry in sorted(merged, key=lambda item: item[:2])]


def arrivals(subs):
    half = MIDDLE_BESIDE
    every = list(range(subs))

    def block(other_column, end, other_side, parts, *directions):
        return [(other_column, end, other_side, part, directions + (SIBLING,)) for part in parts]

    at_end = interleaved(
        block(0, 0, 0, every[:half], BESIDE)
        + block(0, 0, 0, every[half:])
        + block(0, 0, 1, every, BESIDE)
        + block(0, 1, 1, every, BESIDE)
        + block(1, 0, 0, every[half:]),
        block(1, 1, 0, every, PARTNER)
        + block(1, 0, 0, every[:half])
        + block(1, 0, 1, every)
        + block(1, 1, 1, every),
    )
    at_middle = interleaved(
        block(0, 0, 1, every, PARTNER, BESIDE) + block(0, 1, 1, every, PARTNER, BESIDE),
        block(0, 1, 0, every, ACROSS) + block(1, 1, 0, every),
        block(1, 0, 0, every[half:])
        + block(1, 0, 0, every[:half])
        + block(1, 0, 1, every)
        + block(1, 1, 1, every),
    )
    return at_end, at_middle


def complete_groups(entries, group):
    count, found = {}, []
    for step, (other_column, end, other_side, sub, _) in enumerate(entries):
        key = (other_column, end, other_side, sub // group * group)
        count[key] = count.get(key, 0) + 1
        if count[key] == group:
            found.append((step,) + key)
    return found


def proof_kernel(
    rows_hbm, next_hbm, ratio_hbm, behave_ref, action_ref, bucket_ref, table_ref, out_ref,
    held, rows_ref, ratio_ref, row_term, local_sem, send_sem, recv_sem,
):
    z, col = lax.axis_index("row"), lax.axis_index("col")
    x, core = col // 2, col % 2
    is_end = (z == 0) | (z == 3)
    is_middle = jnp.logical_not(is_end)
    side = z // 2
    shard, features = next_hbm.shape
    sub_rows = shard // SUBS
    group = SUBS // 2
    width = 2 * group * sub_rows
    partner = z + 1 - 2 * (z % 2)
    target = {
        PARTNER: (partner, col),
        ACROSS: (3 - z, col),
        BESIDE: (z, (1 - x) * 2 + core),
        SIBLING: (z, x * 2 + 1 - core),
    }

    def device(direction):
        to_row, to_col = target[direction]
        return {"row": to_row, "col": to_col}

    def unit_of(other_column, end, other_side, sub):
        bx = (1 - x) if other_column else x
        bside = (1 - side) if other_side else side
        bz = 3 * bside if end else 1 + bside
        return (bx * 4 + bz) * SUBS + sub

    def part(unit, of_core):
        return held.at[pl.ds(pl.multiple_of((unit * 2 + of_core) * sub_rows, sub_rows), sub_rows), :]

    def transfer(unit, of_core, direction):
        return pltpu.make_async_remote_copy(
            src_ref=part(unit, of_core),
            dst_ref=part(unit, of_core),
            send_sem=send_sem.at[unit, direction],
            recv_sem=recv_sem.at[unit * 2 + of_core],
            device_id=device(direction),
            device_id_type=pl.DeviceIdType.MESH,
        )

    barrier = pltpu.get_barrier_semaphore()

    def greet(direction):
        pl.semaphore_signal(
            barrier, inc=1, device_id=device(direction), device_id_type=pl.DeviceIdType.MESH
        )

    greet(PARTNER)
    greet(BESIDE)
    greet(SIBLING)

    @pl.when(is_middle)
    def _():
        greet(ACROSS)

    mine = (x * 4 + z) * SUBS
    ratio_copy = pltpu.make_async_copy(ratio_hbm, ratio_ref, local_sem.at[0])
    ratio_copy.start()
    next_copies = []
    for sub in range(SUBS):
        next_copies.append(
            pltpu.make_async_copy(
                next_hbm.at[pl.ds(sub * sub_rows, sub_rows), :],
                part(mine + sub, core).at[:, pl.ds(0, features)],
                local_sem.at[2 + sub],
            )
        )
        next_copies[sub].start()
    rows_copy = pltpu.make_async_copy(rows_hbm, rows_ref, local_sem.at[1])
    rows_copy.start()
    columns = jnp.concatenate(
        [
            bucket_ref[...].astype(jnp.float32),
            action_ref[...].astype(jnp.float32),
            behave_ref[...],
            jnp.zeros((5, shard), jnp.float32),
        ],
        axis=0,
    ).T
    buckets = table_ref.shape[0]
    onehot = (columns[:, 0:1] == lax.broadcasted_iota(jnp.int32, (shard, buckets), 1).astype(jnp.float32))
    chosen = lax.dot_general(
        onehot.astype(jnp.float32).astype(jnp.bfloat16),
        table_ref[...].astype(jnp.float32).astype(jnp.bfloat16),
        (((1,), (0,)), ((), ())),
        preferred_element_type=jnp.float32,
    )
    matched = jnp.where(chosen == columns[:, 1:2], 1.0, 0.0)
    importance = matched / columns[:, 2:3]
    ratio_copy.wait()
    residual = ((DISCOUNT * importance - 1.0) * ratio_ref[...]).astype(jnp.bfloat16)
    for sub in range(SUBS):
        own = part(mine + sub, core)
        own[:, features:] = residual[sub * sub_rows:(sub + 1) * sub_rows, :]

    for copy in next_copies:
        copy.wait()
    pl.semaphore_wait(barrier, jnp.where(is_end, 3, 4))

    half = MIDDLE_BESIDE

    @pl.when(is_end)
    def _():
        for sub in range(SUBS):
            transfer(mine + sub, core, BESIDE).start()
            transfer(mine + sub, core, PARTNER).start()

    @pl.when(is_middle)
    def _():
        for sub in range(SUBS):
            transfer(mine + sub, core, PARTNER).start()
            transfer(mine + sub, core, ACROSS).start()
        for sub in range(SUBS):
            transfer(mine + (sub + half) % SUBS, core, BESIDE).start()

    for sub in range(SUBS):
        transfer(mine + sub, core, SIBLING).start()

    fold = KERNEL_SCALE / math.sqrt(features) * math.log2(math.e)
    rows_copy.wait()
    row_count = rows_ref.shape[0]
    tile = min(256, row_count)

    @pl.loop(0, row_count // tile)
    def _(step):
        here = pl.ds(pl.multiple_of(step * tile, tile), tile)
        squares = jnp.square(rows_ref[here, :].astype(jnp.float32))
        row_term[here, :] = fold * (2.0 * features - jnp.sum(squares, axis=1, keepdims=True))
        out_ref[here, :] = jnp.zeros((tile, out_ref.shape[1]), jnp.float32)

    def add_group(unit):
        start = pl.ds(pl.multiple_of(unit * 2 * sub_rows, width), width)
        points = held[start, :features]
        weights = held[start, features:]
        squares = jnp.square(points.astype(jnp.float32))
        lanes = functools.reduce(
            jnp.add, [squares[:, at:at + 128] for at in range(0, features, 128)]
        )
        column_term = fold * jnp.sum(lanes.T, axis=0, keepdims=True)
        inner = lax.dot_general(
            rows_ref[...], points, (((1,), (1,)), ((), ())), preferred_element_type=jnp.float32
        )
        exponent = (2.0 * fold) * inner + (row_term[...] - column_term)
        kernel = jnp.exp2(exponent).astype(jnp.bfloat16)
        out_ref[...] += jnp.dot(kernel, weights, preferred_element_type=jnp.float32)

    at_end, at_middle = arrivals(SUBS)
    groups_of_end, groups_of_middle = complete_groups(at_end, group), complete_groups(at_middle, group)
    waiting = [(1, mine + at) for at in range(0, SUBS, group)]
    for (end_step, *of_end), (middle_step, *of_middle) in zip(
        groups_of_end, groups_of_middle, strict=True
    ):
        first = jnp.where(is_end, unit_of(*of_end), unit_of(*of_middle))
        waiting.append((max(end_step, middle_step) + 1, first))

    def add_next():
        _, first = waiting.pop(0)
        for sub in range(group):
            transfer(first + sub, 1 - core, SIBLING).wait_recv()
        add_group(first)

    passed = []
    for step, (end_entry, middle_entry) in enumerate(zip(at_end, at_middle, strict=True)):
        unit = jnp.where(is_end, unit_of(*end_entry[:4]), unit_of(*middle_entry[:4]))
        transfer(unit, core, SIBLING).wait_recv()
        for direction in (PARTNER, ACROSS, BESIDE, SIBLING):
            in_end, in_middle = direction in end_entry[4], direction in middle_entry[4]
            if in_end and in_middle:
                transfer(unit, core, direction).start()
            elif in_end or in_middle:

                @pl.when(is_end if in_end else is_middle)
                def _():
                    transfer(unit, core, direction).start()

            passed.append((unit, direction, in_end, in_middle))
        if middle_entry[:4] == (0, 1, 1, SUBS - 1):
            for sub in range(half, SUBS):
                beside = unit_of(1, 0, 0, sub)

                @pl.when(is_middle)
                def _():
                    transfer(beside, core, PARTNER).start()

                passed.append((beside, PARTNER, False, True))
        if waiting[0][0] <= step:
            add_next()
    while waiting:
        add_next()

    for sub in range(SUBS):
        for direction in (PARTNER, BESIDE, SIBLING):
            transfer(mine + sub, core, direction).wait_send()

        @pl.when(is_middle)
        def _():
            transfer(mine + sub, core, ACROSS).wait_send()

    for unit, direction, in_end, in_middle in passed:
        if in_end and in_middle:
            transfer(unit, core, direction).wait_send()
        elif in_end or in_middle:

            @pl.when(is_end if in_end else is_middle)
            def _():
                transfer(unit, core, direction).wait_send()


def relayed_body(row_points, next_points, ratio, behave_prob, logged_action, bucket, regime_table):
    rows, features = row_points.shape
    shard, regimes = ratio.shape
    devices = lax.axis_size("row") * lax.axis_size("col")
    columns = devices * shard
    units = devices // 2 * SUBS
    total = pl.pallas_call(
        proof_kernel,
        out_shape=jax.ShapeDtypeStruct((rows, regimes), jnp.float32),
        in_specs=[pl.BlockSpec(memory_space=pltpu.HBM)] * 3
        + [pl.BlockSpec(memory_space=pltpu.VMEM)] * 4,
        out_specs=pl.BlockSpec(memory_space=pltpu.VMEM),
        scratch_shapes=[
            pltpu.VMEM((columns, features + regimes), jnp.bfloat16),
            pltpu.VMEM((rows, features), jnp.bfloat16),
            pltpu.VMEM((shard, regimes), jnp.float32),
            pltpu.VMEM((rows, 1), jnp.float32),
            pltpu.SemaphoreType.DMA((2 + SUBS,)),
            pltpu.SemaphoreType.DMA((units, 4)),
            pltpu.SemaphoreType.DMA((units * 2,)),
        ],
        compiler_params=pltpu.CompilerParams(
            collective_id=0, has_side_effects=True, vmem_limit_bytes=60 * 2**20
        ),
    )(
        row_points,
        next_points,
        ratio,
        behave_prob.reshape(1, shard),
        logged_action.reshape(1, shard),
        bucket.reshape(1, shard),
        regime_table.T,
    )
    return total / float(columns)


def solution(mesh):
    whole_window = mesh.shape["row"] == STEPS == 4 and mesh.shape["col"] == 4
    body = relayed_body if whole_window else gathered_body
    placed = (
        P(("groups", "row", "col"), None),
        P(("groups", "row", "col"), None),
        P(("groups", "row", "col"), None),
        P(("groups", "row", "col")),
        P(("groups", "row", "col")),
        P(("groups", "row", "col")),
        P(),
    )
    return jax.shard_map(
        body,
        mesh=mesh,
        in_specs=placed,
        out_specs=P(("groups", "row", "col"), None),
        check_vma=False,
    )
```

```python
import functools
import math

import jax
import jax.numpy as jnp
from jax import lax
from jax.experimental import pallas as pl
from jax.experimental.pallas import tpu as pltpu
from jax.sharding import PartitionSpec as P

BUCKETS = 64
STEPS = 4


KERNEL_SCALE = 0.5
DISCOUNT = 0.9


def passed_along(block, axis, distance):
    devices = range(lax.axis_size(axis))
    route = [((i - distance) % len(devices), i) for i in devices]
    return lax.ppermute(block, axis, route)


def residual_block(ratio, behave_prob, logged_action, bucket, regime_table):
    onehot = (bucket[:, None] == jnp.arange(BUCKETS, dtype=jnp.int32)[None, :]).astype(jnp.float32)
    chosen = jnp.dot(onehot, regime_table.astype(jnp.float32).T, precision=lax.Precision.HIGHEST)
    matched = (chosen == logged_action.astype(jnp.float32)[:, None]).astype(jnp.float32)
    importance = matched / behave_prob[:, None]
    return ((DISCOUNT * importance - 1.0) * ratio).astype(jnp.bfloat16)


def kernel_tile(row_block, row_norm, column_block):
    features = row_block.shape[1]
    columns = column_block[:, :features]
    residual = column_block[:, features:]
    column_norm = jnp.sum(jnp.square(columns.astype(jnp.float32)), axis=1)
    inner_terms = lax.dot_general(
        row_block, columns, (((1,), (1,)), ((), ())), preferred_element_type=jnp.float32
    )
    coefficient = KERNEL_SCALE / math.sqrt(features)
    exponent = coefficient * (
        2.0 * inner_terms - row_norm[:, None] - column_norm[None, :] + 2.0 * features
    )
    kernel = jnp.exp(exponent).astype(jnp.bfloat16)
    return jnp.dot(kernel, residual, preferred_element_type=jnp.float32)


def gathered_body(row_points, next_points, ratio, behave_prob, logged_action, bucket, regime_table):
    residual = residual_block(ratio, behave_prob, logged_action, bucket, regime_table)
    packed = jnp.concatenate([next_points, residual], axis=1)
    row_norm = jnp.sum(jnp.square(row_points.astype(jnp.float32)), axis=1)
    col_count = lax.axis_size("col")
    local_rows = next_points.shape[0]
    summed = jnp.zeros((row_points.shape[0], ratio.shape[1]), jnp.float32)
    pieces = [packed]
    for offset in range(1, STEPS):
        pieces.append(passed_along(packed, "row", -offset))
    stacked = jnp.stack(pieces, axis=0)
    gathered = lax.all_gather(stacked, "col", axis=1, tiled=True)
    for section in range(STEPS):
        summed = summed + kernel_tile(row_points, row_norm, gathered[section])
    return summed / float(STEPS * col_count * local_rows)


SUBS = 4
MIDDLE_BESIDE = 3
PARTNER, ACROSS, BESIDE, SIBLING = range(4)


def interleaved(*lists):
    merged = []
    for order, entries in enumerate(lists):
        merged += [(place, order, entry) for place, entry in enumerate(entries)]
    return [entry for _, _, entry in sorted(merged, key=lambda item: item[:2])]


def arrivals(subs):
    half = MIDDLE_BESIDE
    every = list(range(subs))

    def block(other_column, end, other_side, parts, *directions):
        return [(other_column, end, other_side, part, directions + (SIBLING,)) for part in parts]

    at_end = interleaved(
        block(0, 0, 0, every[:half], BESIDE)
        + block(0, 0, 0, every[half:])
        + block(0, 0, 1, every, BESIDE)
        + block(0, 1, 1, every, BESIDE)
        + block(1, 0, 0, every[half:]),
        block(1, 1, 0, every, PARTNER)
        + block(1, 0, 0, every[:half])
        + block(1, 0, 1, every)
        + block(1, 1, 1, every),
    )
    at_middle = interleaved(
        block(0, 0, 1, every, PARTNER, BESIDE) + block(0, 1, 1, every, PARTNER, BESIDE),
        block(0, 1, 0, every, ACROSS) + block(1, 1, 0, every),
        block(1, 0, 0, every[half:])
        + block(1, 0, 0, every[:half])
        + block(1, 0, 1, every)
        + block(1, 1, 1, every),
    )
    return at_end, at_middle


def complete_groups(entries, group):
    count, found = {}, []
    for step, (other_column, end, other_side, sub, _) in enumerate(entries):
        key = (other_column, end, other_side, sub // group * group)
        count[key] = count.get(key, 0) + 1
        if count[key] == group:
            found.append((step,) + key)
    return found


def proof_kernel(
    rows_hbm, next_hbm, ratio_hbm, behave_ref, action_ref, bucket_ref, table_ref, out_ref,
    held, rows_ref, ratio_ref, row_term, local_sem, send_sem, recv_sem,
):
    z, col = lax.axis_index("row"), lax.axis_index("col")
    x, core = col // 2, col % 2
    is_end = (z == 0) | (z == 3)
    is_middle = jnp.logical_not(is_end)
    side = z // 2
    shard, features = next_hbm.shape
    sub_rows = shard // SUBS
    group = SUBS // 2
    width = 2 * group * sub_rows
    partner = z + 1 - 2 * (z % 2)
    target = {
        PARTNER: (partner, col),
        ACROSS: (3 - z, col),
        BESIDE: (z, (1 - x) * 2 + core),
        SIBLING: (z, x * 2 + 1 - core),
    }

    def device(direction):
        to_row, to_col = target[direction]
        return {"row": to_row, "col": to_col}

    def unit_of(other_column, end, other_side, sub):
        bx = (1 - x) if other_column else x
        bside = (1 - side) if other_side else side
        bz = 3 * bside if end else 1 + bside
        return (bx * 4 + bz) * SUBS + sub

    def part(unit, of_core):
        return held.at[pl.ds(pl.multiple_of((unit * 2 + of_core) * sub_rows, sub_rows), sub_rows), :]

    def transfer(unit, of_core, direction):
        return pltpu.make_async_remote_copy(
            src_ref=part(unit, of_core),
            dst_ref=part(unit, of_core),
            send_sem=send_sem.at[unit, direction],
            recv_sem=recv_sem.at[unit * 2 + of_core],
            device_id=device(direction),
            device_id_type=pl.DeviceIdType.MESH,
        )

    barrier = pltpu.get_barrier_semaphore()

    def greet(direction):
        pl.semaphore_signal(
            barrier, inc=1, device_id=device(direction), device_id_type=pl.DeviceIdType.MESH
        )

    greet(PARTNER)
    greet(BESIDE)
    greet(SIBLING)

    @pl.when(is_middle)
    def _():
        greet(ACROSS)

    mine = (x * 4 + z) * SUBS
    ratio_copy = pltpu.make_async_copy(ratio_hbm, ratio_ref, local_sem.at[0])
    ratio_copy.start()
    next_copies = []
    for sub in range(SUBS):
        next_copies.append(
            pltpu.make_async_copy(
                next_hbm.at[pl.ds(sub * sub_rows, sub_rows), :],
                part(mine + sub, core).at[:, pl.ds(0, features)],
                local_sem.at[2 + sub],
            )
        )
        next_copies[sub].start()
    rows_copy = pltpu.make_async_copy(rows_hbm, rows_ref, local_sem.at[1])
    rows_copy.start()
    columns = jnp.concatenate(
        [
            bucket_ref[...].astype(jnp.float32),
            action_ref[...].astype(jnp.float32),
            behave_ref[...],
            jnp.zeros((5, shard), jnp.float32),
        ],
        axis=0,
    ).T
    buckets = table_ref.shape[0]
    onehot = (columns[:, 0:1] == lax.broadcasted_iota(jnp.int32, (shard, buckets), 1).astype(jnp.float32))
    chosen = lax.dot_general(
        onehot.astype(jnp.float32).astype(jnp.bfloat16),
        table_ref[...].astype(jnp.float32).astype(jnp.bfloat16),
        (((1,), (0,)), ((), ())),
        preferred_element_type=jnp.float32,
    )
    matched = jnp.where(chosen == columns[:, 1:2], 1.0, 0.0)
    importance = matched / columns[:, 2:3]
    ratio_copy.wait()
    residual = ((DISCOUNT * importance - 1.0) * ratio_ref[...]).astype(jnp.bfloat16)
    for sub in range(SUBS):
        own = part(mine + sub, core)
        own[:, features:] = residual[sub * sub_rows:(sub + 1) * sub_rows, :]

    for copy in next_copies:
        copy.wait()
    pl.semaphore_wait(barrier, jnp.where(is_end, 3, 4))

    half = MIDDLE_BESIDE

    @pl.when(is_end)
    def _():
        for sub in range(SUBS):
            transfer(mine + sub, core, BESIDE).start()
            transfer(mine + sub, core, PARTNER).start()

    @pl.when(is_middle)
    def _():
        for sub in range(SUBS):
            transfer(mine + sub, core, PARTNER).start()
            transfer(mine + sub, core, ACROSS).start()
        for sub in range(SUBS):
            transfer(mine + (sub + half) % SUBS, core, BESIDE).start()

    for sub in range(SUBS):
        transfer(mine + sub, core, SIBLING).start()

    fold = KERNEL_SCALE / math.sqrt(features) * math.log2(math.e)
    row_count = rows_ref.shape[0]
    tile = min(256, row_count)

    def prepare_rows():
        rows_copy.wait()

        @pl.loop(0, row_count // tile)
        def _(step):
            here = pl.ds(pl.multiple_of(step * tile, tile), tile)
            squares = jnp.square(rows_ref[here, :].astype(jnp.float32))
            row_term[here, :] = fold * (2.0 * features - jnp.sum(squares, axis=1, keepdims=True))
            out_ref[here, :] = jnp.zeros((tile, out_ref.shape[1]), jnp.float32)

    def add_group(unit):
        start = pl.ds(pl.multiple_of(unit * 2 * sub_rows, width), width)
        points = held[start, :features]
        weights = held[start, features:]
        squares = jnp.square(points.astype(jnp.float32))
        lanes = functools.reduce(
            jnp.add, [squares[:, at:at + 128] for at in range(0, features, 128)]
        )
        column_term = fold * jnp.sum(lanes.T, axis=0, keepdims=True)
        inner = lax.dot_general(
            rows_ref[...], points, (((1,), (1,)), ((), ())), preferred_element_type=jnp.float32
        )
        exponent = (2.0 * fold) * inner + (row_term[...] - column_term)
        kernel = jnp.exp2(exponent).astype(jnp.bfloat16)
        out_ref[...] += jnp.dot(kernel, weights, preferred_element_type=jnp.float32)

    at_end, at_middle = arrivals(SUBS)
    groups_of_end, groups_of_middle = complete_groups(at_end, group), complete_groups(at_middle, group)
    waiting = [(1, mine + at) for at in range(0, SUBS, group)]
    for (end_step, *of_end), (middle_step, *of_middle) in zip(
        groups_of_end, groups_of_middle, strict=True
    ):
        first = jnp.where(is_end, unit_of(*of_end), unit_of(*of_middle))
        waiting.append((max(end_step, middle_step) + 1, first))

    def add_next():
        _, first = waiting.pop(0)
        for sub in range(group):
            transfer(first + sub, 1 - core, SIBLING).wait_recv()
        add_group(first)

    passed = []
    for step, (end_entry, middle_entry) in enumerate(zip(at_end, at_middle, strict=True)):
        unit = jnp.where(is_end, unit_of(*end_entry[:4]), unit_of(*middle_entry[:4]))
        transfer(unit, core, SIBLING).wait_recv()
        for direction in (PARTNER, ACROSS, BESIDE, SIBLING):
            in_end, in_middle = direction in end_entry[4], direction in middle_entry[4]
            if in_end and in_middle:
                transfer(unit, core, direction).start()
            elif in_end or in_middle:

                @pl.when(is_end if in_end else is_middle)
                def _():
                    transfer(unit, core, direction).start()

            passed.append((unit, direction, in_end, in_middle))
        if middle_entry[:4] == (0, 1, 1, SUBS - 1):
            for sub in range(half, SUBS):
                beside = unit_of(1, 0, 0, sub)

                @pl.when(is_middle)
                def _():
                    transfer(beside, core, PARTNER).start()

                passed.append((beside, PARTNER, False, True))
        if step == 1:
            prepare_rows()
        if waiting[0][0] <= step:
            add_next()
    while waiting:
        add_next()

    for sub in range(SUBS):
        for direction in (PARTNER, BESIDE, SIBLING):
            transfer(mine + sub, core, direction).wait_send()

        @pl.when(is_middle)
        def _():
            transfer(mine + sub, core, ACROSS).wait_send()

    for unit, direction, in_end, in_middle in passed:
        if in_end and in_middle:
            transfer(unit, core, direction).wait_send()
        elif in_end or in_middle:

            @pl.when(is_end if in_end else is_middle)
            def _():
                transfer(unit, core, direction).wait_send()


def relayed_body(row_points, next_points, ratio, behave_prob, logged_action, bucket, regime_table):
    rows, features = row_points.shape
    shard, regimes = ratio.shape
    devices = lax.axis_size("row") * lax.axis_size("col")
    columns = devices * shard
    units = devices // 2 * SUBS
    total = pl.pallas_call(
        proof_kernel,
        out_shape=jax.ShapeDtypeStruct((rows, regimes), jnp.float32),
        in_specs=[pl.BlockSpec(memory_space=pltpu.HBM)] * 3
        + [pl.BlockSpec(memory_space=pltpu.VMEM)] * 4,
        out_specs=pl.BlockSpec(memory_space=pltpu.VMEM),
        scratch_shapes=[
            pltpu.VMEM((columns, features + regimes), jnp.bfloat16),
            pltpu.VMEM((rows, features), jnp.bfloat16),
            pltpu.VMEM((shard, regimes), jnp.float32),
            pltpu.VMEM((rows, 1), jnp.float32),
            pltpu.SemaphoreType.DMA((2 + SUBS,)),
            pltpu.SemaphoreType.DMA((units, 4)),
            pltpu.SemaphoreType.DMA((units * 2,)),
        ],
        compiler_params=pltpu.CompilerParams(
            collective_id=0, has_side_effects=True, vmem_limit_bytes=60 * 2**20
        ),
    )(
        row_points,
        next_points,
        ratio,
        behave_prob.reshape(1, shard),
        logged_action.reshape(1, shard),
        bucket.reshape(1, shard),
        regime_table.T,
    )
    return total / float(columns)


def solution(mesh):
    whole_window = mesh.shape["row"] == STEPS == 4 and mesh.shape["col"] == 4
    body = relayed_body if whole_window else gathered_body
    placed = (
        P(("groups", "row", "col"), None),
        P(("groups", "row", "col"), None),
        P(("groups", "row", "col"), None),
        P(("groups", "row", "col")),
        P(("groups", "row", "col")),
        P(("groups", "row", "col")),
        P(),
    )
    return jax.shard_map(
        body,
        mesh=mesh,
        in_specs=placed,
        out_specs=P(("groups", "row", "col"), None),
        check_vma=False,
    )
```
